128 devices in a mesh: rx: 4 (over x), ry: 2 (over y_hi), node: 16 (over z, y_lo, core).
Axes of the slice: x: 4, y: 4 (y_hi: 2, y_lo: 2; y = y_hi * 2 + y_lo), z: 4, core: 2. Of those that a mesh axis runs over, the one named last changes fastest.
Arguments:
- activations: bfloat16 [8, 6144, 640], P(('rx', 'ry'), 'node'), may hold values from -6 to 6
- output_grad: bfloat16 [8, 6144, 14336], P(('rx', 'ry'), 'node'), may hold values from -48 to 48
- inner_drift: bfloat16 [8, 640, 14336], P(('rx', 'ry'), 'node'), may hold values from -0.1796875 to 0.1796875
- outer_weights: float32 [640, 14336], P('node', ('rx', 'ry')), may hold values from -0.25 to 0.25
- outer_momentum: float32 [640, 14336], P('node', ('rx', 'ry')), may hold values from -0.12 to 0.12
- next_inputs: bfloat16 [8, 6144, 640], P(('rx', 'ry'), 'node'), may hold values from -6 to 6
Outputs:
- new_weights: float32 [640, 14336], P('node', ('rx', 'ry'))
- new_momentum: float32 [640, 14336], P('node', ('rx', 'ry'))
- next_outputs: bfloat16 [8, 6144, 14336], P(('rx', 'ry'), 'node')
The draws below stay inside these ranges and needn't reach their ends.
All inputs are finite; a program needn't handle non-finite values.
Results may differ from the reference program's by a relative error of at most 0.02.
Values may be sent and summed in bfloat16 or wider, within the bound.
A program may use at most 128 MiB of HBM per device.

```python
import jax
import jax.numpy as jnp
from jax import lax

FF = 14336
TOK_DEV = 384
WROWS = 640
REPLICAS = 8
TOKENS_R = 6144
N_NODE = 16


def steps_of(own_key, dims, cuts, low, largest):
    def one(dim, parts):
        steps = jax.random.uniform(jax.random.fold_in(jax.random.fold_in(own_key, 6), dim), (parts,), jnp.float32, low / len(cuts), largest / len(cuts))
        return jnp.repeat(jnp.exp(steps), dims[dim] // parts).reshape((-1,) + (1,) * (len(dims) - dim - 1))

    factor_of = one(*cuts[0])
    for cut in cuts[1:]:
        factor_of = factor_of * one(*cut)
    return factor_of


def centred(rng, shape, width, bound, pieces=(), dtype=jnp.bfloat16):
    level = steps_of(rng, shape, pieces, -0.22, 0.18) if pieces else 1.0
    entries = jax.random.normal(rng, shape, jnp.float32) * width * level
    return jnp.minimum(jnp.maximum(entries, -bound), bound).astype(dtype)


def setup_inputs(seed: int = 0) -> dict:
    splits = jax.random.split(jax.random.key(seed), 7)
    activations = centred(splits[0], (REPLICAS, TOKENS_R, WROWS), 1.0, 6.0, ((0, 8), (1, 16)))
    output_grad = centred(splits[1], (REPLICAS, TOKENS_R, FF), 8.0, 48.0, ((0, 8), (1, 16)))
    inner_drift = centred(splits[2], (REPLICAS, WROWS, FF), 0.03, 0.1796875, ((0, 8), (1, 16)))
    outer_weights = centred(splits[3], (WROWS, FF), WROWS ** -0.5, 0.25, ((0, 16), (1, 8)), jnp.float32)
    outer_momentum = centred(splits[4], (WROWS, FF), 0.02, 0.12, ((0, 16), (1, 8)), jnp.float32)
    next_inputs = centred(splits[5], (REPLICAS, TOKENS_R, WROWS), 1.0, 6.0, ((0, 8), (1, 16)))
    return {"activations": activations, "output_grad": output_grad, "inner_drift": inner_drift, "outer_weights": outer_weights, "outer_momentum": outer_momentum, "next_inputs": next_inputs}


inner_rate = 0.5
outer_rate = 0.7
decay_rate = 0.9


def replica_term(operands):
    inputs_now, grads_now, drift_now = operands
    scale = 1.0 / TOKENS_R
    inputs_grouped = inputs_now.reshape(N_NODE, TOK_DEV, WROWS)
    grads_grouped = grads_now.reshape(N_NODE, TOK_DEV, FF)

    def add_group(summed, pair):
        group_in, group_grad = pair
        product = jnp.dot(group_in.T, group_grad, preferred_element_type=jnp.float32) * scale
        rounded = lax.optimization_barrier(product.astype(jnp.bfloat16))
        return summed + rounded.astype(jnp.float32), None

    start_sum = jnp.zeros((WROWS, FF), jnp.float32)
    grad_sum, _ = lax.scan(add_group, start_sum, (inputs_grouped, grads_grouped))
    return drift_now.astype(jnp.float32) + inner_rate * grad_sum


def reference(activations, output_grad, inner_drift, outer_weights, outer_momentum, next_inputs):
    terms = lax.map(replica_term, (activations, output_grad, inner_drift))
    pseudo_grad = jnp.sum(terms, axis=0) / REPLICAS
    new_momentum = decay_rate * outer_momentum + pseudo_grad
    new_weights = outer_weights - outer_rate * (pseudo_grad + decay_rate * new_momentum)
    weights_bf = new_weights.astype(jnp.bfloat16)

    def forward(inputs_next):
        return jnp.dot(inputs_next, weights_bf, preferred_element_type=jnp.float32).astype(jnp.bfloat16)

    next_outputs = lax.map(forward, next_inputs)
    return new_weights, new_momentum, next_outputs
```

```python
import functools

import jax
import jax.numpy as jnp
from jax import lax
from jax.experimental import pallas as pl
from jax.experimental.pallas import tpu as pltpu
from jax.sharding import PartitionSpec as P

inner_rate = 0.5
outer_rate = 0.7
decay_rate = 0.9

MESH = pl.DeviceIdType.MESH
BF = jnp.bfloat16
F32 = jnp.float32

CHUNKS = (
    (0, 384, (("xyz", 0, 128, 0, 80), ("yzx", 128, 128, 0, 80), ("zxy", 256, 128, 0, 80))),
    (
        384,
        512,
        (
            ("xyz", 384, 128, 0, 80),
            ("yzx", 512, 128, 0, 80),
            ("zxy", 640, 128, 0, 80),
            ("xyz", 768, 128, 0, 32),
            ("yzx", 768, 128, 32, 32),
            ("zxy", 768, 128, 64, 16),
        ),
    ),
)
PARTS = tuple(part for _, _, parts in CHUNKS for part in parts)


def place():
    n = lax.axis_index("node")
    return {
        "x": lax.axis_index("rx"),
        "y": lax.axis_index("ry") * 2 + (n // 2) % 2,
        "z": n // 4,
        "c": n % 2,
    }


def device(at):
    return (at["x"], at["y"] // 2, (at["z"] * 2 + at["y"] % 2) * 2 + at["c"])


def step(at, axis, by):
    return {**at, axis: (at[axis] + by) % 4}


def index(axes, sel):
    def one(axis):
        s = sel.get(axis)
        if s is None:
            return slice(None)
        return pl.ds(2 * s[1], 2) if isinstance(s, tuple) else s

    y = sel.get("y")
    out = [one("x")] if "x" in axes else []
    if "y" in axes:
        out.append(slice(None) if y is None else y[1] if isinstance(y, tuple) else y // 2)
    if "z" in axes:
        out.append(one("z"))
    if "y" in axes:
        out.append(slice(None) if y is None or isinstance(y, tuple) else y % 2)
    return tuple(out)


def dims(axes, tail):
    shape = (4,) if "x" in axes else ()
    shape += (2,) if "y" in axes else ()
    shape += (4,) if "z" in axes else ()
    shape += (2,) if "y" in axes else ()
    return shape + tail


def ordered(axes):
    return "".join(axis for axis in "xyz" if axis in axes)


def sync_kernel(*refs):
    np_ = len(PARTS)
    act, grad, drift, w_in, m_in = refs[:5]
    nw_out, nm_out = refs[5:7]
    w_out = refs[7 : 7 + np_]
    rest = list(refs[7 + np_ :])
    a_own, a_sib, at_buf, dr_own, dr_sib, dr32, ow, om, nw, nm = rest[:10]
    del rest[:10]
    g_buf = [rest.pop(0) for _ in CHUNKS]
    p_buf = [rest.pop(0) for _ in PARTS]
    stage = [rest.pop(0) for _ in PARTS]
    ring = [[[rest.pop(0) for _ in range(3)] for _ in range(3)] for _ in PARTS]
    send, recv, local = rest

    at = place()
    h = at["c"]
    sib = {**at, "c": 1 - h}
    rows_own = pl.multiple_of(h * 40, 8)
    rows_sib = pl.multiple_of((1 - h) * 40, 8)
    count = {"r": 0, "l": 0}
    pending = []

    def remote(src, dst, to):
        k = count["r"]
        count["r"] += 1
        copy = pltpu.make_async_remote_copy(
            src, dst, send.at[k], recv.at[k], device_id=device(to), device_id_type=MESH
        )
        copy.start()
        pending.append(copy)
        return copy

    def near(src, dst):
        k = count["l"]
        count["l"] += 1
        copy = pltpu.make_async_copy(src, dst, local.at[k])
        copy.start()
        return copy

    load_act = near(act.at[0], a_own)
    load_g = []
    for k, (c0, wc, _) in enumerate(CHUNKS):
        load_g.append(
            [
                near(
                    grad.at[0, :, pl.ds(pl.multiple_of(q * 1792 + h * 896 + c0, 128), wc)],
                    g_buf[k].at[q, pl.ds(0, 384)],
                )
                for q in range(8)
            ]
        )
    load_dr = [
        near(drift.at[0, :, pl.ds(pl.multiple_of(q * 1792 + h * 896, 128), 896)], dr_own.at[q])
        for q in range(8)
    ]
    col_own = pl.ds(pl.multiple_of(h * 896, 128), 896)
    col_sib = pl.ds(pl.multiple_of((1 - h) * 896, 128), 896)
    load_ow = near(w_in.at[:, col_own], ow.at[pl.ds(rows_own, 40)])
    load_om = near(m_in.at[:, col_own], om.at[pl.ds(rows_own, 40)])

    barrier = pltpu.get_barrier_semaphore()
    others = [sib] + [step(at, axis, by) for axis in "xyz" for by in (1, 2, 3)]
    for to in others:
        pl.semaphore_signal(barrier, 1, device_id=device(to), device_id_type=MESH)
    pl.semaphore_wait(barrier, len(others))

    send_act = remote(act.at[0], a_sib, sib)
    send_g = []
    for k, (c0, wc, _) in enumerate(CHUNKS):
        send_g.append(
            [
                remote(
                    grad.at[0, :, pl.ds(pl.multiple_of(q * 1792 + (1 - h) * 896 + c0, 128), wc)],
                    g_buf[k].at[q, pl.ds(384, 384)],
                    sib,
                )
                for q in range(8)
            ]
        )
        if k == 0:
            send_dr = [
                remote(
                    drift.at[0, :, pl.ds(pl.multiple_of(q * 1792 + (1 - h) * 896, 128), 896)],
                    dr_sib.at[q],
                    sib,
                )
                for q in range(8)
            ]
    send_ow = remote(w_in.at[:, col_sib], ow.at[pl.ds(rows_own, 40)], sib)
    send_om = remote(m_in.at[:, col_sib], om.at[pl.ds(rows_own, 40)], sib)

    load_act.wait()
    for i in range(5):
        at_buf[pl.ds(i * 128, 128), pl.ds(0, 384)] = a_own[:, pl.ds(i * 128, 128)].T
    send_act.wait_recv()
    for i in range(5):
        at_buf[pl.ds(i * 128, 128), pl.ds(384, 384)] = a_sib[:, pl.ds(i * 128, 128)].T

    scale = inner_rate / (384 * 16)

    def product(k):
        c0, wc, parts = CHUNKS[k]
        for copy in load_g[k]:
            copy.wait()
        for copy in send_g[k]:
            copy.wait_recv()
        if k == 0:
            for copy in load_dr:
                copy.wait()
            for copy in send_dr:
                copy.wait_recv()
            load_ow.wait()
            load_om.wait()
            send_ow.wait_recv()
            send_om.wait_recv()

            @pl.loop(0, 8)
            def _(q):
                dr32[q, pl.ds(rows_own, 40)] = dr_own[q].astype(F32)
                dr32[q, pl.ds(rows_sib, 40)] = dr_sib[q].astype(F32)

        @pl.loop(0, 8)
        def _(q):
            total = jnp.dot(at_buf[...], g_buf[k][q], preferred_element_type=F32)
            value = (total * scale).astype(BF)
            for part in parts:
                order, pc, w, r0, rows = part
                ref = p_buf[PARTS.index(part)]
                block = value[:, pc - c0 : pc - c0 + w].reshape(4, 2, 80, w)
                ref[q // 2, q % 2] = block[:, :, r0 : r0 + rows]
                mine = (q // 2, q % 2, at["z"], at["y"] % 2)
                ref[mine] = (
                    ref[mine].astype(F32) + dr32[q, pl.ds(r0, rows), pl.ds(pc, w)]
                ).astype(BF)

    def tiles(axes, half_axis, half, body):
        n = 4 ** len(axes) // (1 if half_axis is None else 2)

        @pl.loop(0, n)
        def _(i):
            sel = {}
            for axis in axes:
                if axis == half_axis:
                    sel[axis] = 2 * half + i % 2
                    i = i // 2
                else:
                    sel[axis] = i % 4
                    i = i // 4
            body(sel)

    def pipeline(s):
        order, pc, w, r0, rows = PARTS[s]
        p, wo, st = p_buf[s], w_out[s], stage[s]
        fixed = {}
        for phase in range(2):
            axis = order[phase]
            left_axes = ordered(order[phase + 1 :])
            split = order[-1]
            via, from_left, from_right = ring[s][phase]
            m = at[axis]
            right, left = step(at, axis, 1), step(at, axis, 3)

            def block(dest, half):
                return p.at[index("xyz", {**fixed, axis: dest % 4, split: ("half", half)})]

            def part_of(ref, half):
                return ref.at[index(left_axes, {split: ("half", half)})]

            v0 = remote(block(m + 2, 0), part_of(via, 0), right)
            v1 = remote(block(m + 2, 1), part_of(via, 1), left)
            e0 = remote(block(m + 1, 1), part_of(from_left, 1), right)
            e1 = remote(block(m + 3, 0), part_of(from_right, 0), left)
            yield
            v0.wait_recv()
            v1.wait_recv()
            for half, dest in ((0, m + 1), (1, m + 3)):

                def add(sel):
                    i = index("xyz", {**fixed, **sel, axis: dest % 4})
                    p[i] = (p[i].astype(F32) + via[index(left_axes, sel)].astype(F32)).astype(BF)

                tiles(left_axes, split, half, add)
            l0 = remote(block(m + 1, 0), part_of(from_left, 0), right)
            l1 = remote(block(m + 3, 1), part_of(from_right, 1), left)
            yield
            for copy in (e0, e1, l0, l1):
                copy.wait_recv()

            def total(sel):
                i = index("xyz", {**fixed, **sel, axis: m})
                j = index(left_axes, sel)
                p[i] = (
                    p[i].astype(F32) + (from_left[j].astype(F32) + from_right[j].astype(F32))
                ).astype(BF)

            tiles(left_axes, None, 0, total)
            fixed[axis] = m
        axis = order[2]
        bufs = ring[s][2]
        got = [
            remote(
                p.at[index("xyz", {**fixed, axis: (at[axis] + by) % 4})],
                bufs[by - 1],
                step(at, axis, by),
            )
            for by in (1, 2, 3)
        ]
        yield
        for copy in got:
            copy.wait_recv()
        me = {"x": at["x"], "y": at["y"], "z": at["z"]}
        mine = index("xyz", me)
        summed = p[mine].astype(F32)
        for ref in bufs:
            summed = summed + ref[...].astype(F32)
        pseudo = summed * 0.125
        area = (pl.ds(r0, rows), pl.ds(pc, w))
        momentum = decay_rate * om[area] + pseudo
        weights = ow[area] - outer_rate * (pseudo + decay_rate * momentum)
        nm[area] = momentum
        nw[area] = weights
        st[...] = weights.astype(BF)

        def tile(sel):
            return wo.at[(h,) + index("xyz", sel)]

        keep = near(st, tile(me))
        got = [remote(st, tile(me), step(at, axis, by)) for by in (1, 2, 3)]
        yield
        keep.wait()
        for copy in got:
            copy.wait_recv()
        across = []
        for phase in (1, 0):
            axis = order[phase]
            split = order[-1]
            del fixed[axis]
            m = at[axis]
            right, left = step(at, axis, 1), step(at, axis, 3)

            def part(pos, half=None):
                sel = {**fixed, axis: pos % 4}
                if half is not None:
                    sel[split] = ("half", half)
                return tile(sel)

            r = remote(part(m), part(m), right)
            l = remote(part(m), part(m), left)
            if phase == 0:
                across.append(remote(part(m), part(m), sib))
            yield
            r.wait_recv()
            fr = remote(part(m + 3, 0), part(m + 3, 0), right)
            l.wait_recv()
            fl = remote(part(m + 1, 1), part(m + 1, 1), left)
            if phase == 0:
                across.append(remote(part(m + 3), part(m + 3), sib))
                across.append(remote(part(m + 1), part(m + 1), sib))
            yield
            fr.wait_recv()
            fl.wait_recv()
        across.append(remote(part(m + 2), part(m + 2), sib))
        yield
        for copy in across:
            copy.wait_recv()

    runs = []
    first = 0
    for _, _, parts in CHUNKS:
        runs.append([pipeline(first + i) for i in range(len(parts))])
        first += len(parts)

    def go(k, n=1):
        for _ in range(n):
            for run in runs[k]:
                next(run, None)

    schedule(product, go)

    back = [
        remote(nw.at[pl.ds(rows_sib, 40)], nw_out.at[:, col_own], sib),
        remote(nm.at[pl.ds(rows_sib, 40)], nm_out.at[:, col_own], sib),
    ]
    keep = [
        near(nw.at[pl.ds(rows_own, 40)], nw_out.at[:, col_own]),
        near(nm.at[pl.ds(rows_own, 40)], nm_out.at[:, col_own]),
    ]
    for k in range(len(CHUNKS)):
        go(k)
    for copy in keep:
        copy.wait()
    for copy in back:
        copy.wait_recv()
    for copy in pending:
        copy.wait_send()


def schedule(product, go):
    product(0)
    go(0)
    product(1)
    go(0)
    go(1)
    go(0)
    go(0)
    go(0)
    go(1)
    go(0)
    go(0)
    go(1)
    go(0)
    go(1)
    go(0)
    go(1)
    go(1)
    go(0)
    go(1)
    go(1)
    go(0)
    go(1)
    go(1)
    go(1)


def out_kernel(*refs):
    np_ = len(PARTS)
    x_ref = refs[0]
    w_refs = refs[1 : 1 + np_]
    o_ref = refs[1 + np_]
    strips = {}
    for part, ref in zip(PARTS, w_refs):
        strips.setdefault((part[1], part[2]), []).append((part[3], part[4], ref))
    columns = []
    for key in sorted(strips):
        rows = [ref[...].reshape(8, n, key[1]) for _, n, ref in sorted(strips[key], key=lambda t: t[0])]
        block = rows[0] if len(rows) == 1 else jnp.concatenate(rows, axis=1)
        columns.append(block.reshape(640, key[1]))
    weights = jnp.concatenate(columns, axis=1)
    o_ref[...] = jnp.dot(x_ref[...], weights, preferred_element_type=F32).astype(BF)[None]


def local(activations, output_grad, inner_drift, outer_weights, outer_momentum, next_inputs):
    any_ = pl.BlockSpec(memory_space=pl.ANY)
    w_shapes = [
        jax.ShapeDtypeStruct((2,) + dims("xyz", (rows, w)), BF) for _, _, w, _, rows in PARTS
    ]
    scratch = [
        pltpu.VMEM((384, 640), BF),
        pltpu.VMEM((384, 640), BF),
        pltpu.VMEM((640, 768), BF),
        pltpu.VMEM((8, 40, 896), BF),
        pltpu.VMEM((8, 40, 896), BF),
        pltpu.VMEM((8, 80, 896), F32),
    ]
    scratch += [pltpu.VMEM((80, 896), F32)] * 4
    scratch += [pltpu.VMEM((8, 768, wc), BF) for _, wc, _ in CHUNKS]
    scratch += [pltpu.VMEM(dims("xyz", (rows, w)), BF) for _, _, w, _, rows in PARTS]
    scratch += [pltpu.VMEM((rows, w), BF) for _, _, w, _, rows in PARTS]
    for order, _, w, _, rows in PARTS:
        for phase in range(3):
            scratch += [pltpu.VMEM(dims(ordered(order[phase + 1 :]), (rows, w)), BF)] * 3
    n_remote = 1 + 8 * len(CHUNKS) + 8 + 2 + 2 + len(PARTS) * (15 + 3 + 8 + 4)
    n_local = 1 + 8 * len(CHUNKS) + 8 + 2 + 2 + len(PARTS)
    scratch += [
        pltpu.SemaphoreType.DMA((n_remote,)),
        pltpu.SemaphoreType.DMA((n_remote,)),
        pltpu.SemaphoreType.DMA((n_local,)),
    ]
    state = jax.ShapeDtypeStruct((40, 1792), F32)
    results = pl.pallas_call(
        sync_kernel,
        out_shape=[state, state] + w_shapes,
        in_specs=[any_] * 5,
        out_specs=[any_] * (2 + len(PARTS)),
        scratch_shapes=scratch,
        compiler_params=pltpu.CompilerParams(
            collective_id=0, has_side_effects=True, vmem_limit_bytes=60 * 2**20
        ),
        name="sync",
    )(activations, output_grad, inner_drift, outer_weights, outer_momentum)
    new_weights, new_momentum, w_all = results[0], results[1], results[2:]

    def w_spec(part):
        _, _, w, _, rows = part
        return pl.BlockSpec(
            (None, None, None, 4, 2, rows, w), lambda q, h: (h, q // 2, q % 2, 0, 0, 0, 0)
        )

    next_outputs = pl.pallas_call(
        out_kernel,
        out_shape=jax.ShapeDtypeStruct((1, 384, 14336), BF),
        grid=(8, 2),
        in_specs=[pl.BlockSpec((384, 640), lambda q, h: (0, 0))] + [w_spec(p) for p in PARTS],
        out_specs=pl.BlockSpec((1, 384, 896), lambda q, h: (0, 0, q * 2 + h)),
        compiler_params=pltpu.CompilerParams(vmem_limit_bytes=32 * 2**20),
        name="outputs",
    )(next_inputs[0], *w_all)
    return new_weights, new_momentum, next_outputs


def solution(mesh):
    in_specs = (
        P(("rx", "ry"), "node", None),
        P(("rx", "ry"), "node", None),
        P(("rx", "ry"), "node", None),
        P("node", ("rx", "ry")),
        P("node", ("rx", "ry")),
        P(("rx", "ry"), "node", None),
    )
    out_specs = (P("node", ("rx", "ry")), P("node", ("rx", "ry")), P(("rx", "ry"), "node", None))
    return jax.shard_map(local, mesh=mesh, in_specs=in_specs, out_specs=out_specs, check_vma=False)
```

```python
import functools

import jax
import jax.numpy as jnp
from jax import lax
from jax.experimental import pallas as pl
from jax.experimental.pallas import tpu as pltpu
from jax.sharding import PartitionSpec as P

inner_rate = 0.5
outer_rate = 0.7
decay_rate = 0.9

MESH = pl.DeviceIdType.MESH
BF = jnp.bfloat16
F32 = jnp.float32

CHUNKS = (
    (0, 384, (("xyz", 0, 128, 0, 80), ("yzx", 128, 128, 0, 80), ("zxy", 256, 128, 0, 80))),
    (768, 128, (("xyz", 768, 128, 0, 32), ("yzx", 768, 128, 32, 32), ("zxy", 768, 128, 64, 16))),
    (384, 384, (("xyz", 384, 128, 0, 80), ("yzx", 512, 128, 0, 80), ("zxy", 640, 128, 0, 80))),
)
PARTS = tuple(part for _, _, parts in CHUNKS for part in parts)
PLACES = {0: (0, 384), 1: (384, 128)}
ORDER = (
    "p0", "s0", "p1", "s1", "s0", "s0", "s1", "s1", "p2", "s0", "s1", "s0", "s2", "s1", "s0",
    "s2", "s0", "s1", "s2", "s1", "s0", "s2", "s0", "s1", "s2", "s0", "s1", "s2", "s0", "s2",
    "b0", "s0", "s0", "s2", "s1", "s0", "s2", "s1", "s1", "s2", "s2", "s1", "s0", "s1", "l0",
    "s2", "m004", "s1", "m102", "s2", "m046", "m126", "s2", "m168", "m068", "s2",
)
PRODUCTS = tuple(int(word[1]) for word in ORDER if word[0] == "p")


def place():
    n = lax.axis_index("node")
    return {
        "x": lax.axis_index("rx"),
        "y": lax.axis_index("ry") * 2 + (n // 2) % 2,
        "z": n // 4,
        "c": n % 2,
    }


def device(at):
    return (at["x"], at["y"] // 2, (at["z"] * 2 + at["y"] % 2) * 2 + at["c"])


def step(at, axis, by):
    return {**at, axis: (at[axis] + by) % 4}


def index(axes, sel):
    def one(axis):
        s = sel.get(axis)
        if s is None:
            return slice(None)
        return pl.ds(2 * s[1], 2) if isinstance(s, tuple) else s

    y = sel.get("y")
    out = [one("x")] if "x" in axes else []
    if "y" in axes:
        out.append(slice(None) if y is None else y[1] if isinstance(y, tuple) else y // 2)
    if "z" in axes:
        out.append(one("z"))
    if "y" in axes:
        out.append(slice(None) if y is None or isinstance(y, tuple) else y % 2)
    return tuple(out)


def dims(axes, tail):
    shape = (4,) if "x" in axes else ()
    shape += (2,) if "y" in axes else ()
    shape += (4,) if "z" in axes else ()
    shape += (2,) if "y" in axes else ()
    return shape + tail


def ordered(axes):
    return "".join(axis for axis in "xyz" if axis in axes)


def weights_of(parts, refs, q):
    strips = {}
    for part, ref in zip(parts, refs):
        strips.setdefault((part[1], part[2]), []).append((part[3], part[4], ref))
    lanes = []
    for half in range(2):
        for key in sorted(strips):
            rows = [
                ref[half, q // 2, q % 2].reshape(8, n, key[1])
                for _, n, ref in sorted(strips[key], key=lambda t: t[0])
            ]
            block = rows[0] if len(rows) == 1 else jnp.concatenate(rows, axis=1)
            lanes.append(block.reshape(640, key[1]))
    return jnp.concatenate(lanes, axis=1)


def sync_kernel(*refs):
    act, grad, drift, w_in, m_in, x_in = refs[:6]
    nw_out, nm_out, x_buf, o_out = refs[6:10]
    rest = list(refs[10:])
    w_far = [rest.pop(0) for _ in CHUNKS[0][2]]
    w_last = [rest.pop(0) for _ in CHUNKS[2][2]]
    a_own, a_sib, at_buf, dr32, ow, om, nw, nm = rest[:8]
    del rest[:8]
    w_mid = [rest.pop(0) for _ in CHUNKS[1][2]]
    w_out = w_far + w_mid + w_last
    w_load = [rest.pop(0) for _ in CHUNKS[0][2]]
    dr_own = [rest.pop(0) for _ in CHUNKS]
    dr_sib = [rest.pop(0) for _ in CHUNKS]
    g_buf = [rest.pop(0) for _ in CHUNKS]
    p_buf = [rest.pop(0) for _ in PARTS]
    stage = [rest.pop(0) for _ in PARTS]
    ring = [[[rest.pop(0) for _ in range(3)] for _ in range(3)] for _ in PARTS]
    send, recv, local, load, w_sem = rest

    at = place()
    h = at["c"]
    sib = {**at, "c": 1 - h}
    rows_own = pl.multiple_of(h * 40, 8)
    rows_sib = pl.multiple_of((1 - h) * 40, 8)
    count = {"r": 0, "l": 0}
    pending = []

    def remote(src, dst, to, start=True):
        k = count["r"]
        count["r"] += 1
        copy = pltpu.make_async_remote_copy(
            src, dst, send.at[k], recv.at[k], device_id=device(to), device_id_type=MESH
        )
        if start:
            copy.start()
        pending.append(copy)
        return copy

    def near(src, dst):
        k = count["l"]
        count["l"] += 1
        copy = pltpu.make_async_copy(src, dst, local.at[k])
        copy.start()
        return copy

    def columns(q, half, c0, w):
        return pl.ds(pl.multiple_of(q * 1792 + half * 896 + c0, 128), w)

    def chunk_copies(k, q, kind):
        c0, wc, _ = CHUNKS[k]
        i = k * 8 + q
        cols = columns(q, (h, 1 - h)[kind], c0, wc)
        sources = (grad.at[0, :, cols], drift.at[0, :, cols])
        if kind == 0:
            targets = (g_buf[k].at[q, pl.ds(0, 384)], dr_own[k].at[q])
            return [
                pltpu.make_async_copy(sources[j], targets[j], load.at[j, i]) for j in range(2)
            ]
        targets = (g_buf[k].at[q, pl.ds(384, 384)], dr_sib[k].at[q])
        return [
            pltpu.make_async_remote_copy(
                sources[j],
                targets[j],
                load.at[2 + j, i],
                load.at[4 + j, i],
                device_id=device(sib),
                device_id_type=MESH,
            )
            for j in range(2)
        ]

    def start_chunk(k, kind):
        @pl.loop(0, 8)
        def _(q):
            for copy in chunk_copies(k, q, kind):
                copy.start()

    col_own = pl.ds(pl.multiple_of(h * 896, 128), 896)
    col_sib = pl.ds(pl.multiple_of((1 - h) * 896, 128), 896)

    load_act = near(act.at[0], a_own)
    start_chunk(PRODUCTS[0], 0)
    load_x = near(x_in.at[0], x_buf)

    barrier = pltpu.get_barrier_semaphore()
    others = [sib] + [step(at, axis, by) for axis in "xyz" for by in (1, 2, 3)]
    for to in others:
        pl.semaphore_signal(barrier, 1, device_id=device(to), device_id_type=MESH)
    pl.semaphore_wait(barrier, len(others))

    send_act = remote(act.at[0], a_sib, sib)
    start_chunk(PRODUCTS[0], 1)

    load_act.wait()
    for i in range(5):
        at_buf[pl.ds(i * 128, 128), pl.ds(0, 384)] = a_own[:, pl.ds(i * 128, 128)].T
    send_act.wait_recv()
    for i in range(5):
        at_buf[pl.ds(i * 128, 128), pl.ds(384, 384)] = a_sib[:, pl.ds(i * 128, 128)].T

    scale = inner_rate / (384 * 16)

    def product_part(k, first, last):
        c0, wc, parts = CHUNKS[k]

        @pl.loop(first, last)
        def _(q):
            for copy in chunk_copies(k, q, 0):
                copy.wait()
            for copy in chunk_copies(k, q, 1):
                copy.wait_recv()
            dr32[pl.ds(rows_own, 40), pl.ds(0, wc)] = dr_own[k][q].astype(F32)
            dr32[pl.ds(rows_sib, 40), pl.ds(0, wc)] = dr_sib[k][q].astype(F32)
            total = jnp.dot(at_buf[...], g_buf[k][q], preferred_element_type=F32)
            value = (total * scale).astype(BF)
            for part in parts:
                order, pc, w, r0, rows = part
                ref = p_buf[PARTS.index(part)]
                block = value[:, pc - c0 : pc - c0 + w].reshape(4, 2, 80, w)
                ref[q // 2, q % 2] = block[:, :, r0 : r0 + rows]
                mine = (q // 2, q % 2, at["z"], at["y"] % 2)
                ref[mine] = (
                    ref[mine].astype(F32) + dr32[pl.ds(r0, rows), pl.ds(pc - c0, w)]
                ).astype(BF)

    def product(k):
        product_part(k, 0, 4)
        later = PRODUCTS.index(k) + 1
        if later < len(PRODUCTS):
            start_chunk(PRODUCTS[later], 0)
            start_chunk(PRODUCTS[later], 1)
        product_part(k, 4, 8)
        if k == PRODUCTS[0]:
            for copy in state_copies():
                state.append(copy)

    state = []

    def state_copies():
        return (
            near(w_in.at[:, col_own], ow.at[pl.ds(rows_own, 40)]),
            near(m_in.at[:, col_own], om.at[pl.ds(rows_own, 40)]),
            remote(w_in.at[:, col_sib], ow.at[pl.ds(rows_own, 40)], sib),
            remote(m_in.at[:, col_sib], om.at[pl.ds(rows_own, 40)], sib),
        )

    def have_state():
        for i in range(len(state)):
            if i < 2:
                state[i].wait()
            else:
                state[i].wait_recv()
        state.clear()

    def tiles(axes, half_axis, half, body):
        n = 4 ** len(axes) // (1 if half_axis is None else 2)

        @pl.loop(0, n)
        def _(i):
            sel = {}
            for axis in axes:
                if axis == half_axis:
                    sel[axis] = 2 * half + i % 2
                    i = i // 2
                else:
                    sel[axis] = i % 4
                    i = i // 4
            body(sel)

    def pipeline(s):
        order, pc, w, r0, rows = PARTS[s]
        p, wo, st = p_buf[s], w_out[s], stage[s]
        fixed = {}
        for phase in range(2):
            axis = order[phase]
            left_axes = ordered(order[phase + 1 :])
            split = order[-1]
            via, from_left, from_right = ring[s][phase]
            m = at[axis]
            right, left = step(at, axis, 1), step(at, axis, 3)

            def block(dest, half):
                return p.at[index("xyz", {**fixed, axis: dest % 4, split: ("half", half)})]

            def part_of(ref, half):
                return ref.at[index(left_axes, {split: ("half", half)})]

            v0 = remote(block(m + 2, 0), part_of(via, 0), right)
            v1 = remote(block(m + 2, 1), part_of(via, 1), left)
            if phase == 0:
                yield
            e0 = remote(block(m + 1, 1), part_of(from_left, 1), right)
            e1 = remote(block(m + 3, 0), part_of(from_right, 0), left)
            yield
            v0.wait_recv()
            v1.wait_recv()
            for half, dest in ((0, m + 1), (1, m + 3)):

                def add(sel):
                    i = index("xyz", {**fixed, **sel, axis: dest % 4})
                    p[i] = (p[i].astype(F32) + via[index(left_axes, sel)].astype(F32)).astype(BF)

                tiles(left_axes, split, half, add)
            l0 = remote(block(m + 1, 0), part_of(from_left, 0), right)
            l1 = remote(block(m + 3, 1), part_of(from_right, 1), left)
            yield
            for copy in (e0, e1, l0, l1):
                copy.wait_recv()

            def total(sel):
                i = index("xyz", {**fixed, **sel, axis: m})
                j = index(left_axes, sel)
                p[i] = (
                    p[i].astype(F32) + (from_left[j].astype(F32) + from_right[j].astype(F32))
                ).astype(BF)

            tiles(left_axes, None, 0, total)
            fixed[axis] = m
        axis = order[2]
        bufs = ring[s][2]
        got = [
            remote(
                p.at[index("xyz", {**fixed, axis: (at[axis] + by) % 4})],
                bufs[by - 1],
                step(at, axis, by),
            )
            for by in (1, 2, 3)
        ]
        yield
        for copy in got:
            copy.wait_recv()
        have_state()
        me = {"x": at["x"], "y": at["y"], "z": at["z"]}
        mine = index("xyz", me)
        summed = p[mine].astype(F32)
        for ref in bufs:
            summed = summed + ref[...].astype(F32)
        pseudo = summed * 0.125
        area = (pl.ds(r0, rows), pl.ds(pc, w))
        momentum = decay_rate * om[area] + pseudo
        weights = ow[area] - outer_rate * (pseudo + decay_rate * momentum)
        nm[area] = momentum
        nw[area] = weights
        st[...] = weights.astype(BF)

        def tile(sel):
            return wo.at[(h,) + index("xyz", sel)]

        keep = near(st, tile(me))
        got = [remote(st, tile(me), step(at, axis, by)) for by in (1, 2, 3)]
        yield
        keep.wait()
        for copy in got:
            copy.wait_recv()
        split = order[2]
        across = []

        def part(axis, pos, half=None):
            sel = {**fixed, axis: pos % 4}
            if half is not None:
                sel[split] = ("half", half)
            return tile(sel)

        axis = order[1]
        del fixed[axis]
        m = at[axis]
        right, left = step(at, axis, 1), step(at, axis, 3)
        r = remote(part(axis, m), part(axis, m), right)
        l = remote(part(axis, m), part(axis, m), left)
        yield
        r.wait_recv()
        fr = remote(part(axis, m + 3, 0), part(axis, m + 3, 0), right)
        l.wait_recv()
        fl = remote(part(axis, m + 1, 1), part(axis, m + 1, 1), left)
        yield
        fr.wait_recv()
        fl.wait_recv()
        axis = order[0]
        del fixed[axis]
        m = at[axis]
        right, left = step(at, axis, 1), step(at, axis, 3)
        r0_, l1_ = (
            remote(part(axis, m, half), part(axis, m, half), to)
            for half, to in ((0, right), (1, left))
        )
        across.append(remote(part(axis, m), part(axis, m), sib))
        yield
        r1_, l0_ = (
            remote(part(axis, m, half), part(axis, m, half), to)
            for half, to in ((1, right), (0, left))
        )
        yield
        r0_.wait_recv()
        fr = remote(part(axis, m + 3, 0), part(axis, m + 3, 0), right)
        l1_.wait_recv()
        fl = remote(part(axis, m + 1, 1), part(axis, m + 1, 1), left)
        yield
        r1_.wait_recv()
        l0_.wait_recv()
        across.append(remote(part(axis, m + 3), part(axis, m + 3), sib))
        across.append(remote(part(axis, m + 1), part(axis, m + 1), sib))
        yield
        fr.wait_recv()
        fl.wait_recv()
        across.append(remote(part(axis, m + 2), part(axis, m + 2), sib))
        yield
        for copy in across:
            copy.wait_recv()

    runs = []
    first = 0
    for _, _, parts in CHUNKS:
        runs.append([pipeline(first + i) for i in range(len(parts))])
        first += len(parts)

    def go(k, n=1):
        for _ in range(n):
            for run in runs[k]:
                next(run, None)

    def weight_copies(k, q):
        base = sum(len(parts) for _, _, parts in CHUNKS[:k])
        return [
            pltpu.make_async_copy(
                w_out[base + i].at[:, q // 2, q % 2],
                w_load[i].at[:, q // 2, q % 2],
                w_sem.at[k, i * 8 + q],
            )
            for i in range(len(CHUNKS[k][2]))
        ]

    def load_weights(k):
        @pl.loop(0, 8)
        def _(q):
            for copy in weight_copies(k, q):
                copy.start()

    def outputs(k, first, last):
        c0, wc, parts = CHUNKS[k]
        if k == 0 and first == 0:
            load_x.wait()
        refs_of = (w_load, w_mid)[k]
        @pl.loop(first, last)
        def _(q):
            if k == 0:
                for copy in weight_copies(k, q):
                    copy.wait()
            value = jnp.dot(
                x_buf[...], weights_of(parts, refs_of, q), preferred_element_type=F32
            ).astype(BF)
            base, _ = PLACES[k]
            for half in range(2):
                cols = pl.ds(pl.multiple_of((q * 2 + half) * 512 + base, 128), wc)
                o_out[:, cols] = value[:, half * wc : (half + 1) * wc]

    back = []

    def send_back():
        back.append(remote(nw.at[pl.ds(rows_sib, 40)], nw_out.at[:, col_own], sib))
        back.append(remote(nm.at[pl.ds(rows_sib, 40)], nm_out.at[:, col_own], sib))
        nw_out[:, col_own] = nw[pl.ds(rows_own, 40)]
        nm_out[:, col_own] = nm[pl.ds(rows_own, 40)]

    for word in ORDER:
        kind, k = word[0], int(word[1])
        if kind == "p":
            product(k)
        elif kind == "s":
            go(k)
        elif kind == "l":
            load_weights(k)
        elif kind == "m":
            outputs(k, int(word[2]), int(word[3]))
        else:
            send_back()

    for run in sum(runs, []):
        for _ in run:
            pass
    for copy in back:
        copy.wait_recv()
    for copy in pending:
        copy.wait_send()
    for k in range(len(CHUNKS)):

        @pl.loop(0, 8)
        def _(q):
            for copy in chunk_copies(k, q, 1):
                copy.wait_send()


def last_kernel(nw, nm, x, early, w0, w1, w2, nw_out, nm_out, o_out, buf, sem):
    c0, wc, parts = CHUNKS[2]

    def early_copies(q):
        copies = []
        for half in range(2):
            for k, (base, w) in PLACES.items():
                src = pl.ds(pl.multiple_of((q * 2 + half) * 512 + base, 128), w)
                dst = pl.ds(pl.multiple_of(q * 1792 + half * 896 + CHUNKS[k][0], 128), w)
                copies.append(
                    pltpu.make_async_copy(
                        early.at[:, src], o_out.at[0, :, dst], sem.at[2 + q * 6 + half * 2 + k]
                    )
                )
        return copies

    def last_copies(q):
        return [
            pltpu.make_async_copy(
                buf.at[q, :, pl.ds(half * wc, wc)],
                o_out.at[0, :, pl.ds(pl.multiple_of(q * 1792 + half * 896 + c0, 128), wc)],
                sem.at[2 + q * 6 + 4 + half],
            )
            for half in range(2)
        ]

    state = [
        pltpu.make_async_copy(nw, nw_out, sem.at[0]),
        pltpu.make_async_copy(nm, nm_out, sem.at[1]),
    ]
    for copy in state:
        copy.start()

    @pl.loop(0, 8)
    def _(q):
        for copy in early_copies(q):
            copy.start()

    @pl.loop(0, 8)
    def _(q):
        weights = weights_of(parts, (w0, w1, w2), q)
        buf[q] = jnp.dot(x[...], weights, preferred_element_type=F32).astype(BF)
        for copy in last_copies(q):
            copy.start()

    for copy in state:
        copy.wait()

    @pl.loop(0, 8)
    def _(q):
        for copy in early_copies(q) + last_copies(q):
            copy.wait()


def local(activations, output_grad, inner_drift, outer_weights, outer_momentum, next_inputs):
    any_ = pl.BlockSpec(memory_space=pl.ANY)
    vmem = pl.BlockSpec(memory_space=pltpu.VMEM)
    w_shapes = [(2,) + dims("xyz", (rows, w)) for _, _, w, _, rows in PARTS]
    scratch = [
        pltpu.VMEM((384, 640), BF),
        pltpu.VMEM((384, 640), BF),
        pltpu.VMEM((640, 768), BF),
        pltpu.VMEM((80, max(wc for _, wc, _ in CHUNKS)), F32),
    ]
    scratch += [pltpu.VMEM((80, 896), F32)] * 4
    scratch += [pltpu.VMEM(shape, BF) for shape in w_shapes[3:6] + w_shapes[:3]]
    scratch += [pltpu.VMEM((8, 40, wc), BF) for _, wc, _ in CHUNKS] * 2
    scratch += [pltpu.VMEM((8, 768, wc), BF) for _, wc, _ in CHUNKS]
    scratch += [pltpu.VMEM(dims("xyz", (rows, w)), BF) for _, _, w, _, rows in PARTS]
    scratch += [pltpu.VMEM((rows, w), BF) for _, _, w, _, rows in PARTS]
    for order, _, w, _, rows in PARTS:
        for phase in range(3):
            scratch += [pltpu.VMEM(dims(ordered(order[phase + 1 :]), (rows, w)), BF)] * 3
    n_remote = 1 + 2 + 2 + len(PARTS) * 32
    n_local = 2 + 2 + len(PARTS)
    scratch += [
        pltpu.SemaphoreType.DMA((n_remote,)),
        pltpu.SemaphoreType.DMA((n_remote,)),
        pltpu.SemaphoreType.DMA((n_local,)),
        pltpu.SemaphoreType.DMA((6, 8 * len(CHUNKS))),
        pltpu.SemaphoreType.DMA((len(CHUNKS), 8 * 3)),
    ]
    results = pl.pallas_call(
        sync_kernel,
        out_shape=[pltpu.VMEM((40, 1792), F32)] * 2
        + [pltpu.VMEM((384, 640), BF), pltpu.VMEM((384, 16 * 512), BF)]
        + [jax.ShapeDtypeStruct(shape, BF) for shape in w_shapes[:3]]
        + [pltpu.VMEM(shape, BF) for shape in w_shapes[6:]],
        in_specs=[any_] * 6,
        out_specs=[vmem] * 4 + [any_] * 3 + [vmem] * 3,
        scratch_shapes=scratch,
        compiler_params=pltpu.CompilerParams(
            collective_id=0, has_side_effects=True, vmem_limit_bytes=47 * 2**20
        ),
        name="sync",
    )(activations, output_grad, inner_drift, outer_weights, outer_momentum, next_inputs)
    new_weights, new_momentum, inputs_next, early = results[:4]
    state = jax.ShapeDtypeStruct((40, 1792), F32)
    return pl.pallas_call(
        last_kernel,
        out_shape=[state, state, jax.ShapeDtypeStruct((1, 384, 14336), BF)],
        in_specs=[vmem] * 7,
        out_specs=[any_] * 3,
        scratch_shapes=[pltpu.VMEM((8, 384, 768), BF), pltpu.SemaphoreType.DMA((2 + 6 * 8,))],
        compiler_params=pltpu.CompilerParams(vmem_limit_bytes=24 * 2**20),
        name="outputs",
    )(new_weights, new_momentum, inputs_next, early, *results[7:])


def solution(mesh):
    in_specs = (
        P(("rx", "ry"), "node", None),
        P(("rx", "ry"), "node", None),
        P(("rx", "ry"), "node", None),
        P("node", ("rx", "ry")),
        P("node", ("rx", "ry")),
        P(("rx", "ry"), "node", None),
    )
    out_specs = (P("node", ("rx", "ry")), P("node", ("rx", "ry")), P(("rx", "ry"), "node", None))
    return jax.shard_map(local, mesh=mesh, in_specs=in_specs, out_specs=out_specs, check_vma=False)
```

```python
import functools

import jax
import jax.numpy as jnp
from jax import lax
from jax.experimental import pallas as pl
from jax.experimental.pallas import tpu as pltpu
from jax.sharding import PartitionSpec as P

inner_rate = 0.5
outer_rate = 0.7
decay_rate = 0.9

MESH = pl.DeviceIdType.MESH
BF = jnp.bfloat16
F32 = jnp.float32

CHUNKS = (
    (0, 384, (("xyz", 0, 128, 0, 80), ("yzx", 128, 128, 0, 80), ("zxy", 256, 128, 0, 80))),
    (768, 128, (("xyz", 768, 128, 0, 32), ("yzx", 768, 128, 32, 32), ("zxy", 768, 128, 64, 16))),
    (384, 384, (("xyz", 384, 128, 0, 80), ("yzx", 512, 128, 0, 80), ("zxy", 640, 128, 0, 80))),
)
PARTS = tuple(part for _, _, parts in CHUNKS for part in parts)
PLACES = {0: (0, 384), 1: (384, 128)}
ORDER = (
    "p0", "s0", "s0", "p1", "s0", "s1", "s1", "p2", "s0", "s1", "s0", "s2", "s0", "s2", "s0",
    "s2", "s0", "s1", "s2", "s1", "s0", "s2", "s1", "s0", "s1", "s2", "s0", "s1", "s2", "b0",
    "s0", "s1", "s2", "s0", "s0", "s1", "s2", "s1", "s0", "s1", "s2", "s1", "s2", "s1", "m002",
    "s1", "m024", "m102", "s2", "s2", "m048", "s2", "m128", "s2",
)
PRODUCTS = tuple(int(word[1]) for word in ORDER if word[0] == "p")


def place():
    n = lax.axis_index("node")
    return {
        "x": lax.axis_index("rx"),
        "y": lax.axis_index("ry") * 2 + (n // 2) % 2,
        "z": n // 4,
        "c": n % 2,
    }


def device(at):
    return (at["x"], at["y"] // 2, (at["z"] * 2 + at["y"] % 2) * 2 + at["c"])


def step(at, axis, by):
    return {**at, axis: (at[axis] + by) % 4}


def index(axes, sel):
    def one(axis):
        s = sel.get(axis)
        if s is None:
            return slice(None)
        return pl.ds(2 * s[1], 2) if isinstance(s, tuple) else s

    y = sel.get("y")
    out = [one("x")] if "x" in axes else []
    if "y" in axes:
        out.append(slice(None) if y is None else y[1] if isinstance(y, tuple) else y // 2)
    if "z" in axes:
        out.append(one("z"))
    if "y" in axes:
        out.append(slice(None) if y is None or isinstance(y, tuple) else y % 2)
    return tuple(out)


def dims(axes, tail):
    shape = (4,) if "x" in axes else ()
    shape += (2,) if "y" in axes else ()
    shape += (4,) if "z" in axes else ()
    shape += (2,) if "y" in axes else ()
    return shape + tail


def ordered(axes):
    return "".join(axis for axis in "xyz" if axis in axes)


def weights_of(parts, refs, q):
    strips = {}
    for part, ref in zip(parts, refs):
        strips.setdefault((part[1], part[2]), []).append((part[3], part[4], ref))
    lanes = []
    for half in range(2):
        for key in sorted(strips):
            rows = [
                ref[half, q // 2, q % 2].reshape(8, n, key[1])
                for _, n, ref in sorted(strips[key], key=lambda t: t[0])
            ]
            block = rows[0] if len(rows) == 1 else jnp.concatenate(rows, axis=1)
            lanes.append(block.reshape(640, key[1]))
    return jnp.concatenate(lanes, axis=1)


def sync_kernel(*refs):
    act, grad, drift, w_in, m_in, x_in = refs[:6]
    nw_out, nm_out, x_buf, o_out = refs[6:10]
    rest = list(refs[10:])
    w_last = [rest.pop(0) for _ in CHUNKS[2][2]]
    a_own, a_sib, at_buf, dr32, ow, om, nw, nm = rest[:8]
    del rest[:8]
    w_mid = [rest.pop(0) for _ in CHUNKS[1][2]]
    w_first = [rest.pop(0) for _ in CHUNKS[0][2]]
    w_out = w_first + w_mid + w_last
    dr_own = [rest.pop(0) for _ in CHUNKS]
    dr_sib = [rest.pop(0) for _ in CHUNKS]
    g_buf = [rest.pop(0) for _ in CHUNKS]
    p_buf = [rest.pop(0) for _ in PARTS]
    stage = [rest.pop(0) for _ in PARTS]
    ring = [[[rest.pop(0) for _ in range(3)] for _ in range(3)] for _ in PARTS]
    send, recv, local, load = rest

    at = place()
    h = at["c"]
    sib = {**at, "c": 1 - h}
    rows_own = pl.multiple_of(h * 40, 8)
    rows_sib = pl.multiple_of((1 - h) * 40, 8)
    count = {"r": 0, "l": 0}
    pending = []

    def remote(src, dst, to, start=True):
        k = count["r"]
        count["r"] += 1
        copy = pltpu.make_async_remote_copy(
            src, dst, send.at[k], recv.at[k], device_id=device(to), device_id_type=MESH
        )
        if start:
            copy.start()
        pending.append(copy)
        return copy

    def near(src, dst):
        k = count["l"]
        count["l"] += 1
        copy = pltpu.make_async_copy(src, dst, local.at[k])
        copy.start()
        return copy

    def columns(q, half, c0, w):
        return pl.ds(pl.multiple_of(q * 1792 + half * 896 + c0, 128), w)

    def chunk_copies(k, q, kind):
        c0, wc, _ = CHUNKS[k]
        i = k * 8 + q
        cols = columns(q, (h, 1 - h)[kind], c0, wc)
        sources = (grad.at[0, :, cols], drift.at[0, :, cols])
        if kind == 0:
            targets = (g_buf[k].at[q, pl.ds(0, 384)], dr_own[k].at[q])
            return [
                pltpu.make_async_copy(sources[j], targets[j], load.at[j, i]) for j in range(2)
            ]
        targets = (g_buf[k].at[q, pl.ds(384, 384)], dr_sib[k].at[q])
        return [
            pltpu.make_async_remote_copy(
                sources[j],
                targets[j],
                load.at[2 + j, i],
                load.at[4 + j, i],
                device_id=device(sib),
                device_id_type=MESH,
            )
            for j in range(2)
        ]

    def start_chunk(k, kind):
        @pl.loop(0, 8)
        def _(q):
            for copy in chunk_copies(k, q, kind):
                copy.start()

    col_own = pl.ds(pl.multiple_of(h * 896, 128), 896)
    col_sib = pl.ds(pl.multiple_of((1 - h) * 896, 128), 896)

    load_act = near(act.at[0], a_own)
    start_chunk(PRODUCTS[0], 0)
    waiting = [near(x_in.at[0], x_buf)]

    barrier = pltpu.get_barrier_semaphore()
    others = [sib] + [step(at, axis, by) for axis in "xyz" for by in (1, 2, 3)]
    for to in others:
        pl.semaphore_signal(barrier, 1, device_id=device(to), device_id_type=MESH)
    pl.semaphore_wait(barrier, len(others))

    send_act = remote(act.at[0], a_sib, sib)
    start_chunk(PRODUCTS[0], 1)

    load_act.wait()
    for i in range(5):
        at_buf[pl.ds(i * 128, 128), pl.ds(0, 384)] = a_own[:, pl.ds(i * 128, 128)].T
    send_act.wait_recv()
    for i in range(5):
        at_buf[pl.ds(i * 128, 128), pl.ds(384, 384)] = a_sib[:, pl.ds(i * 128, 128)].T

    scale = inner_rate / (384 * 16)

    def product_part(k, first, last):
        c0, wc, parts = CHUNKS[k]

        @pl.loop(first // 2, last // 2)
        def _(x):
            for y in range(2):
                q = 2 * x + y
                for copy in chunk_copies(k, q, 0):
                    copy.wait()
                for copy in chunk_copies(k, q, 1):
                    copy.wait_recv()
            both = jnp.concatenate([g_buf[k][2 * x], g_buf[k][2 * x + 1]], axis=1)
            total = jnp.dot(at_buf[...], both, preferred_element_type=F32)
            value = (total * scale).astype(BF)
            for y in range(2):
                q = 2 * x + y
                dr32[pl.ds(rows_own, 40), pl.ds(0, wc)] = dr_own[k][q].astype(F32)
                dr32[pl.ds(rows_sib, 40), pl.ds(0, wc)] = dr_sib[k][q].astype(F32)
                for part in parts:
                    order, pc, w, r0, rows = part
                    ref = p_buf[PARTS.index(part)]
                    start = y * wc + pc - c0
                    block = value[:, start : start + w].reshape(4, 2, 80, w)
                    ref[x, y] = block[:, :, r0 : r0 + rows]
                    mine = (x, y, at["z"], at["y"] % 2)
                    ref[mine] = (
                        ref[mine].astype(F32) + dr32[pl.ds(r0, rows), pl.ds(pc - c0, w)]
                    ).astype(BF)

    def product(k):
        product_part(k, 0, 4)
        later = PRODUCTS.index(k) + 1
        if later < len(PRODUCTS):
            start_chunk(PRODUCTS[later], 0)
            start_chunk(PRODUCTS[later], 1)
        product_part(k, 4, 8)
        if k == PRODUCTS[0]:
            for copy in state_copies():
                state.append(copy)

    state = []

    def state_copies():
        return (
            near(w_in.at[:, col_own], ow.at[pl.ds(rows_own, 40)]),
            near(m_in.at[:, col_own], om.at[pl.ds(rows_own, 40)]),
            remote(w_in.at[:, col_sib], ow.at[pl.ds(rows_own, 40)], sib),
            remote(m_in.at[:, col_sib], om.at[pl.ds(rows_own, 40)], sib),
        )

    def have_state():
        for i in range(len(state)):
            if i < 2:
                state[i].wait()
            else:
                state[i].wait_recv()
        state.clear()

    def tiles(axes, half_axis, half, body):
        n = 4 ** len(axes) // (1 if half_axis is None else 2)

        @pl.loop(0, n, unroll=min(n, 4))
        def _(i):
            sel = {}
            for axis in axes:
                if axis == half_axis:
                    sel[axis] = 2 * half + i % 2
                    i = i // 2
                else:
                    sel[axis] = i % 4
                    i = i // 4
            body(sel)

    def pipeline(s):
        order, pc, w, r0, rows = PARTS[s]
        p, wo, st = p_buf[s], w_out[s], stage[s]
        fixed = {}
        for phase in range(2):
            axis = order[phase]
            left_axes = ordered(order[phase + 1 :])
            split = order[-1]
            via, from_left, from_right = ring[s][phase]
            m = at[axis]
            right, left = step(at, axis, 1), step(at, axis, 3)

            def block(dest, half):
                return p.at[index("xyz", {**fixed, axis: dest % 4, split: ("half", half)})]

            def part_of(ref, half):
                return ref.at[index(left_axes, {split: ("half", half)})]

            v0 = remote(block(m + 2, 0), part_of(via, 0), right)
            v1 = remote(block(m + 2, 1), part_of(via, 1), left)
            if phase == 0:
                yield
            e0 = remote(block(m + 1, 1), part_of(from_left, 1), right)
            e1 = remote(block(m + 3, 0), part_of(from_right, 0), left)
            yield
            v0.wait_recv()
            v1.wait_recv()
            for half, dest in ((0, m + 1), (1, m + 3)):

                def add(sel):
                    i = index("xyz", {**fixed, **sel, axis: dest % 4})
                    p[i] = p[i] + via[index(left_axes, sel)]

                tiles(left_axes, split, half, add)
            l0 = remote(block(m + 1, 0), part_of(from_left, 0), right)
            l1 = remote(block(m + 3, 1), part_of(from_right, 1), left)
            yield
            for copy in (e0, e1, l0, l1):
                copy.wait_recv()

            def total(sel):
                i = index("xyz", {**fixed, **sel, axis: m})
                j = index(left_axes, sel)
                p[i] = (
                    p[i].astype(F32) + (from_left[j].astype(F32) + from_right[j].astype(F32))
                ).astype(BF)

            tiles(left_axes, None, 0, total)
            fixed[axis] = m
        axis = order[2]
        bufs = ring[s][2]
        got = [
            remote(
                p.at[index("xyz", {**fixed, axis: (at[axis] + by) % 4})],
                bufs[by - 1],
                step(at, axis, by),
            )
            for by in (1, 2, 3)
        ]
        yield
        for copy in got:
            copy.wait_recv()
        have_state()
        me = {"x": at["x"], "y": at["y"], "z": at["z"]}
        mine = index("xyz", me)
        summed = p[mine].astype(F32)
        for ref in bufs:
            summed = summed + ref[...].astype(F32)
        pseudo = summed * 0.125
        area = (pl.ds(r0, rows), pl.ds(pc, w))
        momentum = decay_rate * om[area] + pseudo
        weights = ow[area] - outer_rate * (pseudo + decay_rate * momentum)
        nm[area] = momentum
        nw[area] = weights
        st[...] = weights.astype(BF)

        def tile(sel):
            return wo.at[(h,) + index("xyz", sel)]

        keep = near(st, tile(me))
        got = [remote(st, tile(me), step(at, axis, by)) for by in (1, 2, 3)]
        yield
        keep.wait()
        for copy in got:
            copy.wait_recv()
        split = order[2]
        across = []

        def part(axis, pos, half=None):
            sel = {**fixed, axis: pos % 4}
            if half is not None:
                sel[split] = ("half", half)
            return tile(sel)

        axis = order[1]
        del fixed[axis]
        m = at[axis]
        right, left = step(at, axis, 1), step(at, axis, 3)
        r = remote(part(axis, m), part(axis, m), right)
        l = remote(part(axis, m), part(axis, m), left)
        yield
        r.wait_recv()
        fr = remote(part(axis, m + 3, 0), part(axis, m + 3, 0), right)
        l.wait_recv()
        fl = remote(part(axis, m + 1, 1), part(axis, m + 1, 1), left)
        yield
        fr.wait_recv()
        fl.wait_recv()
        axis = order[0]
        del fixed[axis]
        m = at[axis]
        right, left = step(at, axis, 1), step(at, axis, 3)
        r0_, l1_ = (
            remote(part(axis, m, half), part(axis, m, half), to)
            for half, to in ((0, right), (1, left))
        )
        across.append(remote(part(axis, m), part(axis, m), sib))
        yield
        r1_, l0_ = (
            remote(part(axis, m, half), part(axis, m, half), to)
            for half, to in ((1, right), (0, left))
        )
        yield
        r0_.wait_recv()
        fr = remote(part(axis, m + 3, 0), part(axis, m + 3, 0), right)
        l1_.wait_recv()
        fl = remote(part(axis, m + 1, 1), part(axis, m + 1, 1), left)
        yield
        r1_.wait_recv()
        l0_.wait_recv()
        across.append(remote(part(axis, m + 3), part(axis, m + 3), sib))
        across.append(remote(part(axis, m + 1), part(axis, m + 1), sib))
        yield
        fr.wait_recv()
        fl.wait_recv()
        across.append(remote(part(axis, m + 2), part(axis, m + 2), sib))
        yield
        for copy in across:
            copy.wait_recv()

    runs = []
    first = 0
    for _, _, parts in CHUNKS:
        runs.append([pipeline(first + i) for i in range(len(parts))])
        first += len(parts)

    def go(k, n=1):
        for _ in range(n):
            for run in runs[k]:
                next(run, None)

    def outputs(k, first, last):
        c0, wc, parts = CHUNKS[k]
        while waiting:
            waiting.pop().wait()
        refs_of = (w_first, w_mid)[k]
        @pl.loop(first, last)
        def _(q):
            value = jnp.dot(
                x_buf[...], weights_of(parts, refs_of, q), preferred_element_type=F32
            ).astype(BF)
            base, _ = PLACES[k]
            for half in range(2):
                cols = pl.ds(pl.multiple_of((q * 2 + half) * 512 + base, 128), wc)
                o_out[:, cols] = value[:, half * wc : (half + 1) * wc]

    back = []

    def send_back():
        back.append(remote(nw.at[pl.ds(rows_sib, 40)], nw_out.at[:, col_own], sib))
        back.append(remote(nm.at[pl.ds(rows_sib, 40)], nm_out.at[:, col_own], sib))
        nw_out[:, col_own] = nw[pl.ds(rows_own, 40)]
        nm_out[:, col_own] = nm[pl.ds(rows_own, 40)]

    for word in ORDER:
        kind, k = word[0], int(word[1])
        if kind == "p":
            product(k)
        elif kind == "s":
            go(k)
        elif kind == "m":
            outputs(k, int(word[2]), int(word[3]))
        else:
            send_back()

    for run in sum(runs, []):
        for _ in run:
            pass
    for copy in back:
        copy.wait_recv()
    for copy in pending:
        copy.wait_send()
    for k in range(len(CHUNKS)):

        @pl.loop(0, 8)
        def _(q):
            for copy in chunk_copies(k, q, 1):
                copy.wait_send()


def last_kernel(nw, nm, x, early, w0, w1, w2, nw_out, nm_out, o_out, buf, sem):
    c0, wc, parts = CHUNKS[2]

    def early_copies(q):
        copies = []
        for half in range(2):
            for k, (base, w) in PLACES.items():
                src = pl.ds(pl.multiple_of((q * 2 + half) * 512 + base, 128), w)
                dst = pl.ds(pl.multiple_of(q * 1792 + half * 896 + CHUNKS[k][0], 128), w)
                copies.append(
                    pltpu.make_async_copy(
                        early.at[:, src], o_out.at[0, :, dst], sem.at[2 + q * 6 + half * 2 + k]
                    )
                )
        return copies

    def last_copies(q):
        return [
            pltpu.make_async_copy(
                buf.at[q, :, pl.ds(half * wc, wc)],
                o_out.at[0, :, pl.ds(pl.multiple_of(q * 1792 + half * 896 + c0, 128), wc)],
                sem.at[2 + q * 6 + 4 + half],
            )
            for half in range(2)
        ]

    state = [
        pltpu.make_async_copy(nw, nw_out, sem.at[0]),
        pltpu.make_async_copy(nm, nm_out, sem.at[1]),
    ]
    for copy in state:
        copy.start()

    @pl.loop(0, 8)
    def _(q):
        for copy in early_copies(q):
            copy.start()

    @pl.loop(0, 8, unroll=4)
    def _(q):
        weights = weights_of(parts, (w0, w1, w2), q)
        buf[q] = jnp.dot(x[...], weights, preferred_element_type=F32).astype(BF)
        for copy in last_copies(q):
            copy.start()

    for copy in state:
        copy.wait()

    @pl.loop(0, 8)
    def _(q):
        for copy in early_copies(q) + last_copies(q):
            copy.wait()


def local(activations, output_grad, inner_drift, outer_weights, outer_momentum, next_inputs):
    any_ = pl.BlockSpec(memory_space=pl.ANY)
    vmem = pl.BlockSpec(memory_space=pltpu.VMEM)
    w_shapes = [(2,) + dims("xyz", (rows, w)) for _, _, w, _, rows in PARTS]
    scratch = [
        pltpu.VMEM((384, 640), BF),
        pltpu.VMEM((384, 640), BF),
        pltpu.VMEM((640, 768), BF),
        pltpu.VMEM((80, max(wc for _, wc, _ in CHUNKS)), F32),
    ]
    scratch += [pltpu.VMEM((80, 896), F32)] * 4
    scratch += [pltpu.VMEM(shape, BF) for shape in w_shapes[3:6] + w_shapes[:3]]
    scratch += [pltpu.VMEM((8, 40, wc), BF) for _, wc, _ in CHUNKS] * 2
    scratch += [pltpu.VMEM((8, 768, wc), BF) for _, wc, _ in CHUNKS]
    scratch += [pltpu.VMEM(dims("xyz", (rows, w)), BF) for _, _, w, _, rows in PARTS]
    scratch += [pltpu.VMEM((rows, w), BF) for _, _, w, _, rows in PARTS]
    for order, _, w, _, rows in PARTS:
        for phase in range(3):
            scratch += [pltpu.VMEM(dims(ordered(order[phase + 1 :]), (rows, w)), BF)] * 3
    n_remote = 1 + 2 + 2 + len(PARTS) * 32
    n_local = 2 + 2 + len(PARTS)
    scratch += [
        pltpu.SemaphoreType.DMA((n_remote,)),
        pltpu.SemaphoreType.DMA((n_remote,)),
        pltpu.SemaphoreType.DMA((n_local,)),
        pltpu.SemaphoreType.DMA((6, 8 * len(CHUNKS))),
    ]
    results = pl.pallas_call(
        sync_kernel,
        out_shape=[pltpu.VMEM((40, 1792), F32)] * 2
        + [pltpu.VMEM((384, 640), BF), pltpu.VMEM((384, 16 * 512), BF)]
        + [pltpu.VMEM(shape, BF) for shape in w_shapes[6:]],
        in_specs=[any_] * 6,
        out_specs=[vmem] * 7,
        scratch_shapes=scratch,
        compiler_params=pltpu.CompilerParams(
            collective_id=0, has_side_effects=True, vmem_limit_bytes=47 * 2**20
        ),
        name="sync",
    )(activations, output_grad, inner_drift, outer_weights, outer_momentum, next_inputs)
    new_weights, new_momentum, inputs_next, early = results[:4]
    state = jax.ShapeDtypeStruct((40, 1792), F32)
    return pl.pallas_call(
        last_kernel,
        out_shape=[state, state, jax.ShapeDtypeStruct((1, 384, 14336), BF)],
        in_specs=[vmem] * 7,
        out_specs=[any_] * 3,
        scratch_shapes=[pltpu.VMEM((8, 384, 768), BF), pltpu.SemaphoreType.DMA((2 + 6 * 8,))],
        compiler_params=pltpu.CompilerParams(vmem_limit_bytes=24 * 2**20),
        name="outputs",
    )(new_weights, new_momentum, inputs_next, early, *results[4:])


def solution(mesh):
    in_specs = (
        P(("rx", "ry"), "node", None),
        P(("rx", "ry"), "node", None),
        P(("rx", "ry"), "node", None),
        P("node", ("rx", "ry")),
        P("node", ("rx", "ry")),
        P(("rx", "ry"), "node", None),
    )
    out_specs = (P("node", ("rx", "ry")), P("node", ("rx", "ry")), P(("rx", "ry"), "node", None))
    return jax.shard_map(local, mesh=mesh, in_specs=in_specs, out_specs=out_specs, check_vma=False)
```
